128 devices in a mesh: segment: 8 (over y_lo, z), dp: 16 (over y_hi, x, core).
Axes of the slice: x: 4, y: 4 (y_hi: 2, y_lo: 2; y = y_hi * 2 + y_lo), z: 4, core: 2. Of those that a mesh axis runs over, the one named last changes fastest.
Arguments:
- tokens: bfloat16 [4, 512, 6144], P(None, 'dp'), may hold values from -18 to 18
- norm_gain: bfloat16 [6144], replicated, may hold values from 0.099609375 to 1.8984375
- router_weight: bfloat16 [6144, 8], replicated, may hold values from -0.078125 to 0.078125
- expert_ids: int32 [4, 512, 2], P(None, 'dp'), may hold values from 0 to 7, all different within a row; in each aligned block of 32 rows (0 to 31, 32 to 63, ..., all dimensions but the last counted through in order) at most 12 rows name the same one
- w_gate: bfloat16 [8, 6144, 8192], P('segment', None, 'dp'), may hold values from -0.078125 to 0.078125
- w_up: bfloat16 [8, 6144, 8192], P('segment', None, 'dp'), may hold values from -0.078125 to 0.078125
- w_down: bfloat16 [8, 8192, 6144], P('segment', 'dp'), may hold values from -0.0625 to 0.0625
Outputs:
- scored: bfloat16 [4, 512, 6144], P(None, 'dp', 'segment')
The draws below stay inside these ranges and needn't reach their ends.
Inputs may be any that keep to these rules, and one draw needn't show every extreme that they name: `expert_ids`: each token names two different experts. In each micro-batch the 32 rows of one device name each expert at most 12 times, and in every draw some expert is named exactly 12 times by some device's rows.
All inputs are finite; a program needn't handle non-finite values.
Results may differ from the reference program's by a relative error of at most 0.0035.
Values may be sent and summed in bfloat16 or wider, within the bound.
A program may use at most 128 MiB of HBM per device.

```python
import math
import jax
import jax.numpy as jnp
import numpy as np
from jax import lax

D = 6144
FF = 8192
MICRO = 4
TOK_DEV = 32
EXPERTS = 8
TOKENS = 512
CAP = 12
N_DP = 16


def draw_tokens(key, part):
    base_key, row_key = jax.random.split(key, 2)
    base = jnp.clip(jax.random.normal(base_key, (MICRO, TOKENS, D), jnp.float32), -6.0, 6.0)
    row_scale = jnp.exp(jax.random.uniform(row_key, (MICRO, TOKENS, 1), jnp.float32, math.log(0.3), math.log(3.0)))
    values = base * row_scale
    return values.astype(jnp.bfloat16)


def level_of(rng, extent, cuts, low, top_value):
    def one(dim, shards_of):
        draws = jax.random.uniform(jax.random.fold_in(jax.random.fold_in(rng, 6), dim), (shards_of,), jnp.float32, low / len(cuts), top_value / len(cuts))
        return jnp.repeat(jnp.exp(draws), extent[dim] // shards_of).reshape((-1,) + (1,) * (len(extent) - dim - 1))

    gain = one(*cuts[0])
    for cut in cuts[1:]:
        gain = gain * one(*cut)
    return gain


def shared_out(rng, own, number, rows, amount, top, reach, skew):
    order = jax.random.permutation(rng, amount)
    heavy_load, usual = load_shares(amount, rows * top, reach, skew, True), load_shares(amount, rows * top, reach, skew, False)
    places = jnp.arange(amount)

    def named(tallies, rotation):
        used = int((tallies > 0).sum())
        fixed = max(1, used // 4)
        moved = fixed + (places - fixed + rotation * (used - fixed)) % max(1, amount - fixed)
        return jnp.zeros((amount,), jnp.int32).at[order[jnp.where(places < fixed, places, moved)]].set(jnp.asarray(tallies, jnp.int32))

    tallies = jnp.where(number % 4 == 0, named(heavy_load, number // 4), named(usual, number - number // 4 - 1))
    mixed = jax.random.permutation(jax.random.fold_in(own, 3), amount)
    giver, receiver = mixed[0:amount // 2 * 2:2], mixed[1:amount // 2 * 2:2]
    slack = jnp.minimum(tallies[giver] - 1, reach - tallies[receiver]) // 2
    slack = jnp.where((giver == order[0]) | (receiver == order[0]) | (tallies[receiver] == 0), 0, jnp.maximum(slack, 0))
    moved = jax.random.randint(jax.random.fold_in(own, 4), (amount // 2,), 0, 1 << 20) % (slack + 1)
    tallies = tallies.at[giver].add(-moved).at[receiver].add(moved)
    items = jnp.searchsorted(jnp.cumsum(tallies), jnp.arange(rows * top), side="right").astype(jnp.int32)
    grid = items.reshape(top, rows).T
    grid = grid[jax.random.permutation(jax.random.fold_in(own, 1), rows)]
    rotation = jax.random.randint(jax.random.fold_in(own, 2), (rows, 1), 0, top)
    return jnp.take_along_axis(grid, (jnp.arange(top)[None, :] + rotation) % top, axis=1)


def load_shares(count, total, limit, slope, full):
    portions = [(1 << 20) // math.isqrt(standing ** slope) + 1 for standing in range(1, count + 1)]
    largest = limit if full else min(limit, max(-(-total // count), total * portions[0] // sum(portions)))
    least = 1 if total - largest >= count - 1 else 0
    given, surplus = [largest] + [least] * (count - 1), total - largest - least * (count - 1)
    while surplus > 0:
        free = [i for i in range(1, count) if given[i] < largest] or [i for i in range(1, count) if given[i] < limit]
        pool, left = sum([portions[i] for i in free]), surplus
        for i in free:
            addition = min(limit - given[i], max(1, left * portions[i] // pool), surplus)
            given[i] = given[i] + addition
            surplus = surplus - addition
    return np.array(given)


def gaussian(stream_key, shape, width, limit, pieces=(), held_as=jnp.bfloat16):
    level = level_of(stream_key, shape, pieces, -0.22, 0.18) if pieces else 1.0
    values = jax.random.normal(stream_key, shape, jnp.float32) * width * level
    return jnp.minimum(jnp.maximum(values, -limit), limit).astype(held_as)


def setup_inputs(seed: int = 0) -> dict:
    key_of = jax.random.split(jax.random.key(seed), 8)
    tokens = draw_tokens(jax.random.fold_in(key_of[7], 71), 0)
    norm_gain = jnp.clip(1.0 + 0.18 * jax.random.normal(key_of[1], (D,), jnp.float32), 0.099609375, 1.8984375).astype(jnp.bfloat16)
    router_weight = gaussian(key_of[2], (D, EXPERTS), D ** -0.5, 0.078125)
    expert_ids_keys = jax.random.split(jax.random.fold_in(key_of[3], 1), MICRO * TOKENS // TOK_DEV)
    expert_ids_turns = jax.random.permutation(jax.random.fold_in(key_of[3], 3), MICRO * TOKENS // TOK_DEV)
    expert_ids = jax.vmap(lambda own, number: shared_out(jax.random.fold_in(key_of[3], 2), own, number, TOK_DEV, EXPERTS, 2, CAP, 2))(expert_ids_keys, expert_ids_turns).reshape((MICRO, TOKENS, 2))
    w_gate = gaussian(key_of[4], (EXPERTS, D, FF), D ** -0.5, 0.078125, ((0, 8), (2, 16)))
    w_up = gaussian(key_of[5], (EXPERTS, D, FF), D ** -0.5, 0.078125, ((0, 8), (2, 16)))
    w_down = gaussian(key_of[6], (EXPERTS, FF, D), FF ** -0.5, 0.0625, ((0, 8), (1, 16)))
    return dict(tokens=tokens, norm_gain=norm_gain, router_weight=router_weight, expert_ids=expert_ids, w_gate=w_gate, w_up=w_up, w_down=w_down)


epsilon = 1e-05

def rms_normed(tokens, norm_gain):
    widened = tokens.astype(jnp.float32)
    inverse_rms = lax.rsqrt(lax.optimization_barrier(jnp.mean(widened * widened, axis=-1, keepdims=True)) + epsilon)
    return (widened, (widened * inverse_rms * norm_gain.astype(jnp.float32)).astype(jnp.bfloat16))

def pair_gates(pair_ids, logits):
    expert_range = jnp.arange(logits.shape[-1], dtype=jnp.int32)
    first_logit = lax.optimization_barrier(jnp.sum(jnp.where(pair_ids[..., 0:1] == expert_range, logits, 0.0), axis=-1))
    second_logit = lax.optimization_barrier(jnp.sum(jnp.where(pair_ids[..., 1:2] == expert_range, logits, 0.0), axis=-1))
    return (jax.nn.sigmoid(first_logit - second_logit), jax.nn.sigmoid(second_logit - first_logit))

def expert_weight(pair_ids, first_gate, second_gate, expert):
    return jnp.where(pair_ids[..., 0] == expert, first_gate, 0.0) + jnp.where(pair_ids[..., 1] == expert, second_gate, 0.0)

def slot_table(pair_ids, expert, slot_count):
    chosen = jnp.any(pair_ids == expert, axis=-1)
    hit_count = chosen.astype(jnp.int32)
    position = jnp.cumsum(hit_count, axis=-1) - hit_count
    slot_range = jnp.arange(slot_count, dtype=jnp.int32)
    dispatch = chosen[..., None, :] & (position[..., None, :] == slot_range[:, None])
    return (position, dispatch)

def reference(tokens, norm_gain, router_weight, expert_ids, w_gate, w_up, w_down):
    widened, normed = rms_normed(tokens, norm_gain)
    logits = jnp.dot(normed.reshape(-1, D), router_weight, preferred_element_type=jnp.float32)
    logits = logits.reshape(MICRO, TOKENS, EXPERTS)
    first_gate, second_gate = pair_gates(expert_ids, logits)
    block_ids = expert_ids.reshape(MICRO, N_DP, TOK_DEV, 2)
    block_rows = normed.reshape(MICRO, N_DP, TOK_DEV, D).astype(jnp.float32)
    unit_count = FF // N_DP

    def add_expert(summed, expert):
        position, dispatch = slot_table(block_ids, expert, CAP)
        dispatch_float = dispatch.astype(jnp.float32)
        routed = jnp.einsum('mgct,mgtf->mgcf', dispatch_float, block_rows).astype(jnp.bfloat16)
        row_block = routed.reshape(-1, D)
        gate_proj = jnp.dot(row_block, w_gate[expert], preferred_element_type=jnp.float32)
        up_proj = jnp.dot(row_block, w_up[expert], preferred_element_type=jnp.float32)
        hidden = (jax.nn.silu(gate_proj) * up_proj).astype(jnp.bfloat16)
        down_matrix = w_down[expert]

        def add_units(accumulated, shard):
            units = lax.dynamic_slice_in_dim(hidden, shard * unit_count, unit_count, 1)
            down_rows = lax.dynamic_slice_in_dim(down_matrix, shard * unit_count, unit_count, 0)
            partial_rows = jnp.dot(units, down_rows, preferred_element_type=jnp.float32)
            return (accumulated + partial_rows, None)
        expert_out, _ = lax.scan(add_units, jnp.zeros((row_block.shape[0], D), jnp.float32), jnp.arange(N_DP, dtype=jnp.int32))
        expert_out = expert_out.reshape(MICRO, N_DP, CAP, D)
        placed = jnp.einsum('mgct,mgcf->mgtf', dispatch_float, expert_out, precision=lax.Precision.HIGHEST)
        weight = expert_weight(expert_ids, first_gate, second_gate, expert).reshape(MICRO, N_DP, TOK_DEV, 1)
        return (summed + weight * placed, None)
    summed, _ = lax.scan(add_expert, jnp.zeros((MICRO, N_DP, TOK_DEV, D), jnp.float32), jnp.arange(EXPERTS, dtype=jnp.int32))
    return (widened + summed.reshape(MICRO, TOKENS, D)).astype(jnp.bfloat16)
```

```python
import functools

import jax
import jax.numpy as jnp
from jax import lax
from jax.experimental import pallas as pl
from jax.experimental.pallas import tpu as pltpu
from jax.sharding import PartitionSpec as P

MESH = pl.DeviceIdType.MESH
F32 = jnp.float32
BF16 = jnp.bfloat16
EPSILON = 1e-05

D = 6144
UNITS = 512
TOK = 128
CAP = 12
CHUNKS = 3
ROWS = 256
TILE = 768
TILES = D // TILE
STEPS = CHUNKS * TILES
RING = 8
LAG_PAIR, LAG_FAR, LAG_NEAR, LAG_ROW = 2, 5, 8, 11
HALF = D // 2


def rows_at(ref_index, count):
    return pl.ds(pl.multiple_of(ref_index, 16), count)


def kernel(
    tok_ref, gain_ref, router_ref, ids_ref, gate_hbm, up_hbm, down_hbm, out_ref,
    gate_w, up_w, down_w, normed, x_buf, hid, acc, pair_out, pair_in, chip_sum,
    first_out, far_in, second_out, near_in, row_sum, row_out, row_in, last_out, last_in,
    load_sem, ag_send, ag_recv, pair_s, pair_r, far_s, far_r, edge_s, near_s, near_r,
    row_s, row_r, last_s, last_r,
):
    s = lax.axis_index("segment")
    d = lax.axis_index("dp")
    core = d % 2
    x = (d // 2) % 4
    yh = d // 8

    def at_x(shift):
        return (s, yh * 8 + ((x + shift + 4) % 4) * 2 + core)

    across = (s, (d + 8) % 16)
    sibling = (s, yh * 8 + x * 2 + 1 - core)

    loads = [
        pltpu.make_async_copy(gate_hbm, gate_w, load_sem.at[0]),
        pltpu.make_async_copy(up_hbm, up_w, load_sem.at[1]),
        pltpu.make_async_copy(down_hbm, down_w, load_sem.at[2]),
    ]
    barrier = pltpu.get_barrier_semaphore()
    partners = [at_x(1), at_x(-1), across, sibling] + [((s + j) % 8, d) for j in range(1, 8)]
    for partner in partners:
        pl.semaphore_signal(barrier, inc=1, device_id=partner, device_id_type=MESH)
    for load in loads:
        load.start()

    def norm_rows(i, _):
        at = rows_at(i * 16, 16)
        wide = tok_ref[at, :].astype(F32)
        inverse = lax.rsqrt(jnp.mean(wide * wide, axis=-1, keepdims=True) + EPSILON)
        normed[at, :] = (wide * inverse * gain_ref[...].astype(F32)).astype(BF16)
        return 0

    lax.fori_loop(0, TOK // 16, norm_rows, 0)

    first_id = ids_ref[:, 0:1]
    second_id = ids_ref[:, 1:2]
    expert = lax.broadcasted_iota(jnp.int32, (TOK, 8), 1)
    chosen = ((first_id == expert) | (second_id == expert)).astype(F32)
    row = lax.broadcasted_iota(jnp.int32, (TOK, TOK), 0)
    col = lax.broadcasted_iota(jnp.int32, (TOK, TOK), 1)
    earlier = ((col < row) & ((col >> 5) == (row >> 5))).astype(F32)
    position = jnp.dot(
        earlier.astype(BF16), chosen.astype(BF16), preferred_element_type=F32
    )
    micro_base = ((lax.broadcasted_iota(jnp.int32, (TOK, 1), 0) >> 5) * CAP).astype(F32)
    own_slot = micro_base + jnp.sum(
        jnp.where(expert == s, position, 0.0), axis=-1, keepdims=True
    )
    named_here = (first_id == s) | (second_id == s)
    slot_range = col.astype(F32)
    placed = jnp.where(named_here & (own_slot == slot_range), 1.0, 0.0)
    dispatch = placed.T[0:48, :].astype(BF16)

    own_row = core * 128 + x * 32 + yh * 16

    def route(j, _):
        cols = pl.ds(pl.multiple_of(j * TILE, TILE), TILE)
        rows = jnp.dot(dispatch, normed[:, cols], preferred_element_type=F32).astype(BF16)
        for c in range(CHUNKS):
            x_buf[c, rows_at(own_row, 16), cols] = rows[c * 16 : (c + 1) * 16]
        return 0

    lax.fori_loop(0, TILES, route, 0)

    def pair_of(shift):
        return core * 128 + ((x + shift + 4) % 4) * 32

    low, high = pl.ds(0, HALF), pl.ds(HALF, HALF)

    def gather(c, kind):
        block = x_buf.at[c, rows_at(own_row, 16)]
        other = x_buf.at[c, rows_at(pair_of(0) + (1 - yh) * 16, 16)]
        ref, to = {
            0: lambda: (block, at_x(1)),
            1: lambda: (block, at_x(-1)),
            2: lambda: (block, across),
            3: lambda: (other, at_x(1)),
            4: lambda: (other, at_x(-1)),
            5: lambda: (x_buf.at[c, rows_at(pair_of(-1), 32), low], at_x(1)),
            6: lambda: (x_buf.at[c, rows_at(pair_of(1), 32), high], at_x(-1)),
            7: lambda: (x_buf.at[c, rows_at(pair_of(0), 32)], sibling),
            8: lambda: (x_buf.at[c, rows_at(pair_of(-1), 32)], sibling),
            9: lambda: (x_buf.at[c, rows_at(pair_of(1), 32)], sibling),
            10: lambda: (x_buf.at[c, rows_at(pair_of(2), 32)], sibling),
        }[kind]()
        return pltpu.make_async_remote_copy(
            src_ref=ref, dst_ref=ref, send_sem=ag_send.at[c, kind], recv_sem=ag_recv.at[c, kind],
            device_id=to, device_id_type=MESH,
        )

    def start_own(c):
        for kind in (2, 0, 1):
            gather(c, kind).start()

    def pass_row(c):
        gather(c, 2).wait_recv()
        for kind in (3, 4, 7):
            gather(c, kind).start()

    def pass_near(c):
        for waits, starts in (((0, 3), (5, 8)), ((1, 4), (6, 9))):
            for kind in waits:
                gather(c, kind).wait_recv()
            for kind in starts:
                gather(c, kind).start()

    def pass_far(c):
        gather(c, 5).wait_recv()
        gather(c, 6).wait_recv()
        gather(c, 10).start()

    def gathered(c):
        for kind in (7, 8, 9, 10):
            gather(c, kind).wait_recv()

    pl.semaphore_wait(barrier, len(partners))
    start_own(0)
    start_own(1)

    logits = jnp.dot(normed[...], router_ref[...], preferred_element_type=F32)
    first_logit = jnp.sum(jnp.where(expert == first_id, logits, 0.0), axis=-1, keepdims=True)
    second_logit = jnp.sum(jnp.where(expert == second_id, logits, 0.0), axis=-1, keepdims=True)
    first_gate = jax.nn.sigmoid(first_logit - second_logit)
    second_gate = jax.nn.sigmoid(second_logit - first_logit)

    pass_row(0)
    pass_near(0)
    start_own(2)
    pass_row(1)
    pass_far(0)
    pass_near(1)
    pass_row(2)
    for load in loads:
        load.wait()

    def remote(src, dst, send, recv, to):
        return pltpu.make_async_remote_copy(
            src_ref=src, dst_ref=dst, send_sem=send, recv_sem=recv, device_id=to, device_id_type=MESH
        )

    def way(n):
        return 1 - 2 * (n % 2)

    def pair_copy(n):
        return remote(pair_out.at[n % RING], pair_in.at[n], pair_s.at[n % RING], pair_r.at[n], sibling)

    def far_copy(n):
        return remote(first_out.at[n % RING, 0], far_in.at[n], far_s.at[n % RING], far_r.at[n], at_x(way(n)))

    def edge_copy(n):
        return remote(first_out.at[n % RING, 1], near_in.at[n, 1], edge_s.at[n % RING], near_r.at[n, 1], at_x(-way(n)))

    def near_copy(n):
        return remote(second_out.at[n % RING], near_in.at[n, 0], near_s.at[n % RING], near_r.at[n, 0], at_x(way(n)))

    def row_copy(n):
        return remote(row_out.at[n % RING], row_in.at[n], row_s.at[n % RING], row_r.at[n], across)

    def last_copy(n, source, to):
        c = n // TILES
        return remote(
            last_out.at[n % RING], last_in.at[c, rows_at(source * 16, 16)], last_s.at[n % RING],
            last_r.at[c, source], (to, d),
        )

    def tile_of(n):
        return (n % TILES + s + 1) % TILES

    def quarter(shift):
        return rows_at(((x + shift + 4) % 4) * 32, 32)

    def hidden_units(c):
        gathered(c)

        def part(j, _):
            cols = pl.ds(pl.multiple_of(j * 256, 256), 256)
            rows = x_buf[c]
            g = jnp.dot(rows, gate_w[:, cols], preferred_element_type=F32)
            u = jnp.dot(rows, up_w[:, cols], preferred_element_type=F32)
            hid[:, cols] = (g * jax.nn.sigmoid(g) * u).astype(BF16)
            return 0

        lax.fori_loop(0, UNITS // 256, part, 0)

    def step(n, _):
        @pl.when(n < STEPS)
        def _():
            c = n // TILES

            @pl.when(n % TILES == 0)
            def _():
                hidden_units(c)

            @pl.when(n == 0)
            def _():
                pass_far(1)
                pass_near(2)

            @pl.when(n == 4)
            def _():
                pass_far(2)

            cols = pl.ds(pl.multiple_of(tile_of(n) * TILE, TILE), TILE)
            acc[n % 3] = jnp.dot(hid[...], down_w[:, cols], preferred_element_type=F32)

            @pl.when(n >= RING)
            def _():
                pair_copy(n - RING).wait_send()

            pair_out[n % RING] = acc[n % 3, rows_at((1 - core) * 128, 128), :].astype(BF16)
            pair_copy(n).start()

        m = n - LAG_PAIR

        @pl.when((m >= 0) & (m < STEPS))
        def _():
            @pl.when(m >= RING)
            def _():
                far_copy(m - RING).wait_send()
                edge_copy(m - RING).wait_send()

            pair_copy(m).wait_recv()
            chip_sum[m % RING] = acc[m % 3, rows_at(core * 128, 128), :] + pair_in[m].astype(F32)
            first_out[m % RING, 0] = chip_sum[m % RING, quarter(2), :].astype(BF16)
            far_copy(m).start()
            first_out[m % RING, 1] = chip_sum[m % RING, quarter(-way(m)), :].astype(BF16)
            edge_copy(m).start()

        p = n - LAG_FAR

        @pl.when((p >= 0) & (p < STEPS))
        def _():
            @pl.when(p >= RING)
            def _():
                near_copy(p - RING).wait_send()

            far_copy(p).wait_recv()
            second_out[p % RING] = (
                chip_sum[p % RING, quarter(way(p)), :] + far_in[p].astype(F32)
            ).astype(BF16)
            near_copy(p).start()

        q = n - LAG_NEAR

        @pl.when((q >= 0) & (q < STEPS))
        def _():
            @pl.when(q >= RING)
            def _():
                row_copy(q - RING).wait_send()

            edge_copy(q).wait_recv()
            near_copy(q).wait_recv()
            row_sum[q % RING] = (
                chip_sum[q % RING, quarter(0), :]
                + near_in[q, 0].astype(F32)
                + near_in[q, 1].astype(F32)
            )
            row_out[q % RING] = row_sum[q % RING, rows_at((1 - yh) * 16, 16), :].astype(BF16)
            row_copy(q).start()

        r = n - LAG_ROW

        @pl.when(r >= 0)
        def _():
            row_copy(r).wait_recv()
            total = row_sum[r % RING, rows_at(yh * 16, 16), :] + row_in[r].astype(F32)

            @pl.when(r % TILES == TILES - 1)
            def _():
                last_in[r // TILES, rows_at(s * 16, 16), :] = total

            @pl.when(r % TILES != TILES - 1)
            def _():
                @pl.when(r >= RING)
                def _():
                    last_copy(r - RING, s, tile_of(r)).wait_send()

                last_out[r % RING] = total
                last_copy(r, s, tile_of(r)).start()

        return 0

    lax.fori_loop(0, STEPS + LAG_ROW, step, 0)

    position_first = jnp.sum(jnp.where(expert == first_id, position, 0.0), axis=-1, keepdims=True)
    position_second = jnp.sum(jnp.where(expert == second_id, position, 0.0), axis=-1, keepdims=True)

    def place_of(expert_id, where):
        slot = (micro_base + where).astype(jnp.int32)
        return (slot >> 4) * 128 + expert_id * 16 + (slot & 15)

    first_place = place_of(first_id, position_first)
    second_place = place_of(second_id, position_second)
    first_sum = jnp.zeros((TOK, TILE), F32)
    second_sum = jnp.zeros((TOK, TILE), F32)
    for c in range(CHUNKS):
        for j in range(1, 8):
            last_copy(c * TILES, (s + j) % 8, s).wait_recv()
        block = last_in[c]
        coarse = block.astype(BF16)
        fine = (block - coarse.astype(F32)).astype(BF16)
        pick_first = jnp.where(first_place == col + c * 128, 1.0, 0.0).astype(BF16)
        pick_second = jnp.where(second_place == col + c * 128, 1.0, 0.0).astype(BF16)
        for part in (coarse, fine):
            first_sum += jnp.dot(pick_first, part, preferred_element_type=F32)
            second_sum += jnp.dot(pick_second, part, preferred_element_type=F32)
    own_cols = pl.ds(pl.multiple_of(s * TILE, TILE), TILE)
    out_ref[...] = (
        tok_ref[:, own_cols].astype(F32) + (first_gate * first_sum + second_gate * second_sum)
    ).astype(BF16)

    for c in range(CHUNKS):
        for kind in range(11):
            gather(c, kind).wait_send()

    def drain(i, _):
        n = STEPS - RING + i
        pair_copy(n).wait_send()
        far_copy(n).wait_send()
        edge_copy(n).wait_send()
        near_copy(n).wait_send()
        row_copy(n).wait_send()

        @pl.when(i < RING - 1)
        def _():
            last_copy(n, s, tile_of(n)).wait_send()

        return 0

    lax.fori_loop(0, RING, drain, 0)


def per_device(tokens, norm_gain, router_weight, expert_ids, w_gate, w_up, w_down):
    vmem = pl.BlockSpec(memory_space=pltpu.VMEM)
    anywhere = pl.BlockSpec(memory_space=pl.ANY)
    dma = pltpu.SemaphoreType.DMA
    out = pl.pallas_call(
        kernel,
        out_shape=jax.ShapeDtypeStruct((TOK, TILE), BF16),
        in_specs=[vmem] * 4 + [anywhere] * 3,
        out_specs=vmem,
        scratch_shapes=[
            pltpu.VMEM((D, UNITS), BF16),
            pltpu.VMEM((D, UNITS), BF16),
            pltpu.VMEM((UNITS, D), BF16),
            pltpu.VMEM((TOK, D), BF16),
            pltpu.VMEM((CHUNKS, ROWS, D), BF16),
            pltpu.VMEM((ROWS, UNITS), BF16),
            pltpu.VMEM((3, ROWS, TILE), F32),
            pltpu.VMEM((RING, 128, TILE), BF16),
            pltpu.VMEM((STEPS, 128, TILE), BF16),
            pltpu.VMEM((RING, 128, TILE), F32),
            pltpu.VMEM((RING, 2, 32, TILE), BF16),
            pltpu.VMEM((STEPS, 32, TILE), BF16),
            pltpu.VMEM((RING, 32, TILE), BF16),
            pltpu.VMEM((STEPS, 2, 32, TILE), BF16),
            pltpu.VMEM((RING, 32, TILE), F32),
            pltpu.VMEM((RING, 16, TILE), BF16),
            pltpu.VMEM((STEPS, 16, TILE), BF16),
            pltpu.VMEM((RING, 16, TILE), F32),
            pltpu.VMEM((CHUNKS, 128, TILE), F32),
            dma((3,)),
            dma((CHUNKS, 11)), dma((CHUNKS, 11)),
            dma((RING,)), dma((STEPS,)),
            dma((RING,)), dma((STEPS,)),
            dma((RING,)), dma((RING,)), dma((STEPS, 2)),
            dma((RING,)), dma((STEPS,)),
            dma((RING,)), dma((CHUNKS, 8)),
        ],
        compiler_params=pltpu.CompilerParams(
            collective_id=0, has_side_effects=True, vmem_limit_bytes=61 * 2**20
        ),
        cost_estimate=pl.CostEstimate(flops=15 * 10**9, bytes_accessed=22 * 10**6, transcendentals=0),
    )(
        tokens.reshape(TOK, D), norm_gain.reshape(1, D), router_weight, expert_ids.reshape(TOK, 2),
        w_gate[0], w_up[0], w_down[0],
    )
    return out.reshape(4, 32, TILE)


def solution(mesh):
    placed = (
        P(None, "dp", None),
        P(),
        P(),
        P(None, "dp", None),
        P("segment", None, "dp"),
        P("segment", None, "dp"),
        P("segment", "dp", None),
    )
    return jax.shard_map(
        per_device, mesh=mesh, in_specs=placed, out_specs=P(None, "dp", "segment"), check_vma=False
    )
```

```python
import functools

import jax
import jax.numpy as jnp
from jax import lax
from jax.experimental import pallas as pl
from jax.experimental.pallas import tpu as pltpu
from jax.sharding import PartitionSpec as P

MESH = pl.DeviceIdType.MESH
F32 = jnp.float32
BF16 = jnp.bfloat16
EPSILON = 1e-05

D = 6144
UNITS = 512
TOK = 128
CAP = 12
CHUNKS = 3
ROWS = 256
TILE = 768
TILES = D // TILE
STEPS = CHUNKS * TILES
RING = 8
KEEP = 12
LAG_PAIR, LAG_FAR, LAG_NEAR, LAG_ROW = 2, 6, 10, 14
HALF = D // 2
LATE = 2560
MIDDLE = (D + LATE) // 2
ROW_TILES = 2


def rows_at(ref_index, count):
    return pl.ds(pl.multiple_of(ref_index, 16), count)


def kernel(
    tok_ref, gain_ref, router_ref, ids_ref, gate_hbm, up_hbm, down_hbm, out_ref,
    gate_w, up_w, down_w, normed, x_buf, hid, acc, pair_out, pair_in, chip_sum,
    first_out, far_in, second_out, near_in, row_sum, row_out, row_in, rows_out, rows_in,
    last_out, last_in, scored,
    load_sem, ag_send, ag_recv, pair_s, pair_r, far_s, far_r, edge_s, near_s, near_r,
    row_s, row_r, rows_s, rows_r, last_s, last_r,
):
    s = lax.axis_index("segment")
    d = lax.axis_index("dp")
    core = d % 2
    x = (d // 2) % 4
    yh = d // 8

    def at_x(shift):
        return (s, yh * 8 + ((x + shift + 4) % 4) * 2 + core)

    across = (s, (d + 8) % 16)
    sibling = (s, yh * 8 + x * 2 + 1 - core)

    loads = [
        pltpu.make_async_copy(gate_hbm, gate_w, load_sem.at[0]),
        pltpu.make_async_copy(up_hbm, up_w, load_sem.at[1]),
        pltpu.make_async_copy(down_hbm, down_w, load_sem.at[2]),
    ]
    barrier = pltpu.get_barrier_semaphore()
    partners = [at_x(1), at_x(-1), across, sibling] + [((s + j) % 8, d) for j in range(1, 8)]
    for partner in partners:
        pl.semaphore_signal(barrier, inc=1, device_id=partner, device_id_type=MESH)
    for load in loads:
        load.start()

    def id_column(which):
        eye = lax.broadcasted_iota(jnp.int32, (32, 32), 0) == lax.broadcasted_iota(
            jnp.int32, (32, 32), 1
        )
        columns = [
            jnp.sum(
                jnp.where(eye, ids_ref[m, which : which + 1, :].astype(F32), 0.0),
                axis=-1,
                keepdims=True,
            )
            for m in range(4)
        ]
        return jnp.concatenate(columns, axis=0).astype(jnp.int32)

    first_id = id_column(0)
    second_id = id_column(1)
    expert = lax.broadcasted_iota(jnp.int32, (TOK, 8), 1)
    chosen = ((first_id == expert) | (second_id == expert)).astype(F32)
    row = lax.broadcasted_iota(jnp.int32, (TOK, TOK), 0)
    col = lax.broadcasted_iota(jnp.int32, (TOK, TOK), 1)
    earlier = ((col < row) & ((col >> 5) == (row >> 5))).astype(F32)
    position = jnp.dot(
        earlier.astype(BF16), chosen.astype(BF16), preferred_element_type=F32
    )
    micro_base = ((lax.broadcasted_iota(jnp.int32, (TOK, 1), 0) >> 5) * CAP).astype(F32)
    own_slot = micro_base + jnp.sum(
        jnp.where(expert == s, position, 0.0), axis=-1, keepdims=True
    )
    named_here = (first_id == s) | (second_id == s)
    slot_range = col.astype(F32)
    dispatch = jnp.where(named_here & (own_slot == slot_range), 1.0, 0.0).T

    def norm(first, count):
        gain = gain_ref[...].astype(F32).reshape(1, D)

        def norm_rows(i, _):
            at = rows_at(first + i * 16, 16)
            wide = tok_ref[at, :].astype(F32)
            inverse = lax.rsqrt(jnp.mean(wide * wide, axis=-1, keepdims=True) + EPSILON)
            normed[at, :] = (wide * inverse * gain).astype(BF16)
            return 0

        lax.fori_loop(0, count // 16, norm_rows, 0)

    own_row = core * 128 + x * 32 + yh * 16

    def route(c):
        pick = dispatch[c * 16 : (c + 1) * 16, c * 32 : c * 32 + 64].astype(BF16)

        def columns(j, _):
            cols = pl.ds(pl.multiple_of(j * TILE, TILE), TILE)
            x_buf[c, rows_at(own_row, 16), cols] = jnp.dot(
                pick, normed[c * 32 : c * 32 + 64, cols], preferred_element_type=F32
            ).astype(BF16)
            return 0

        lax.fori_loop(0, TILES, columns, 0)

    def pair_of(shift):
        return core * 128 + ((x + shift + 4) % 4) * 32

    def gather(c, kind):
        def block(shift, row):
            return x_buf.at[c, rows_at(pair_of(shift) + row * 16, 16)]

        def part(shift, row, start, stop):
            return x_buf.at[c, rows_at(pair_of(shift) + row * 16, 16), pl.ds(start, stop - start)]

        def pair(shift):
            return x_buf.at[c, rows_at(pair_of(shift), 32)]

        ref, to = {
            0: lambda: (block(0, yh), at_x(1)),
            1: lambda: (block(0, yh), at_x(-1)),
            2: lambda: (block(0, yh), across),
            3: lambda: (part(0, 1 - yh, LATE, D), at_x(1)),
            4: lambda: (part(0, 1 - yh, LATE, D), at_x(-1)),
            5: lambda: (part(-1, yh, 0, HALF), at_x(1)),
            6: lambda: (part(1, yh, HALF, D), at_x(-1)),
            7: lambda: (part(-1, 1 - yh, LATE, MIDDLE), at_x(1)),
            8: lambda: (part(1, 1 - yh, MIDDLE, D), at_x(-1)),
            9: lambda: (part(-1, yh, 0, LATE), across),
            10: lambda: (part(1, yh, 0, LATE), across),
            11: lambda: (part(2, yh, 0, LATE), across),
            12: lambda: (pair(0), sibling),
            13: lambda: (pair(-1), sibling),
            14: lambda: (pair(1), sibling),
            15: lambda: (pair(2), sibling),
        }[kind]()
        return pltpu.make_async_remote_copy(
            src_ref=ref, dst_ref=ref, send_sem=ag_send.at[c, kind], recv_sem=ag_recv.at[c, kind],
            device_id=to, device_id_type=MESH,
        )

    def go_on(c, waits, starts):
        for kind in waits:
            gather(c, kind).wait_recv()
        for kind in starts:
            gather(c, kind).start()

    def own_rows(c):
        go_on(c, (), (0, 1, 2))

    def pass_first(c):
        go_on(c, (0,), (5, 9))
        go_on(c, (1,), (6, 10))
        go_on(c, (2,), (3, 4, 12))

    def pass_near(c):
        go_on(c, (3,), (7,))
        go_on(c, (4,), (8,))
        go_on(c, (5, 6), (11,))

    def pass_late(c):
        go_on(c, (9,), (13,))
        go_on(c, (10,), (14,))

    def pass_far(c):
        go_on(c, (7, 8, 11), (15,))

    def gathered(c):
        go_on(c, (12, 13, 14, 15), ())

    norm(0, 64)
    route(0)
    pl.semaphore_wait(barrier, len(partners))
    own_rows(0)
    norm(64, 32)
    route(1)
    own_rows(1)
    norm(96, 32)
    route(2)

    logits = lax.dot_general(
        normed[...], router_ref[...], (((1,), (1,)), ((), ())), preferred_element_type=F32
    )
    first_logit = jnp.sum(jnp.where(expert == first_id, logits, 0.0), axis=-1, keepdims=True)
    second_logit = jnp.sum(jnp.where(expert == second_id, logits, 0.0), axis=-1, keepdims=True)
    first_gate = jax.nn.sigmoid(first_logit - second_logit)
    second_gate = jax.nn.sigmoid(second_logit - first_logit)

    pass_first(0)
    pass_near(0)
    pass_first(1)
    own_rows(2)
    pass_late(0)
    pass_far(0)
    pass_near(1)
    for load in loads:
        load.wait()

    def remote(src, dst, send, recv, to):
        return pltpu.make_async_remote_copy(
            src_ref=src, dst_ref=dst, send_sem=send, recv_sem=recv, device_id=to, device_id_type=MESH
        )

    def way(n):
        return 1 - 2 * (n % 2)

    def pair_copy(n):
        return remote(pair_out.at[n % RING], pair_in.at[n], pair_s.at[n % RING], pair_r.at[n], sibling)

    def far_copy(n):
        return remote(first_out.at[n % RING, 0], far_in.at[n], far_s.at[n % RING], far_r.at[n], at_x(way(n)))

    def edge_copy(n):
        return remote(first_out.at[n % RING, 1], near_in.at[n, 1], edge_s.at[n % RING], near_r.at[n, 1], at_x(-way(n)))

    def near_copy(n):
        return remote(second_out.at[n % RING], near_in.at[n, 0], near_s.at[n % RING], near_r.at[n, 0], at_x(way(n)))

    def row_copy(n):
        return remote(row_out.at[n % RING], row_in.at[n], row_s.at[n % RING], row_r.at[n], across)

    def row_first(n):
        return (n % TILES == 2) | (n % TILES == 5)

    def row_place(n):
        return (n // TILES) * ROW_TILES + (n % TILES) // 4

    def rows_copy(n):
        return remote(rows_out.at[(n % TILES) // 4], rows_in.at[row_place(n)], rows_s.at[(n % TILES) // 4], rows_r.at[row_place(n)], across)

    top = pl.ds(0, 16)

    def far_block(n):
        return remote(first_out.at[n % RING, 0, top], far_in.at[n, top], far_s.at[n % RING], far_r.at[n], at_x(way(n)))

    def edge_block(n):
        return remote(first_out.at[n % RING, 1, top], near_in.at[n, 1, top], edge_s.at[n % RING], near_r.at[n, 1], at_x(-way(n)))

    def near_block(n):
        return remote(second_out.at[n % RING, top], near_in.at[n, 0, top], near_s.at[n % RING], near_r.at[n, 0], at_x(way(n)))

    def last_copy(n, source, to):
        c = n // TILES
        return remote(
            last_out.at[n % RING], last_in.at[c, rows_at(source * 16, 16)], last_s.at[n % RING],
            last_r.at[c, source], (to, d),
        )

    def tile_of(n):
        return (n % TILES + s + 1) % TILES

    def quarter(shift):
        return rows_at(((x + shift + 4) % 4) * 32, 32)

    def own_block(shift):
        return rows_at(((x + shift + 4) % 4) * 32 + yh * 16, 16)

    def hidden_units(c):
        gathered(c)

        def part(j, _):
            cols = pl.ds(pl.multiple_of(j * 256, 256), 256)
            rows = x_buf[c]
            g = jnp.dot(rows, gate_w[:, cols], preferred_element_type=F32)
            u = jnp.dot(rows, up_w[:, cols], preferred_element_type=F32)
            hid[:, cols] = (g * jax.nn.sigmoid(g) * u).astype(BF16)
            return 0

        lax.fori_loop(0, UNITS // 256, part, 0)

    def place_of(expert_id):
        where = jnp.sum(jnp.where(expert == expert_id, position, 0.0), axis=-1, keepdims=True)
        slot = (micro_base + where).astype(jnp.int32)
        return (slot >> 4) * 128 + expert_id * 16 + (slot & 15)

    first_place = place_of(first_id)
    second_place = place_of(second_id)
    own_cols = pl.ds(pl.multiple_of(s * TILE, TILE), TILE)
    scored[...] = tok_ref[:, own_cols].astype(F32)

    def combine(c):
        for j in range(1, 8):
            last_copy(c * TILES, (s + j) % 8, s).wait_recv()
        block = last_in[c]
        coarse = block.astype(BF16)
        fine = (block - coarse.astype(F32)).astype(BF16)
        toks = slice(c * 32, c * 32 + 64)
        added = 0.0
        for place, gate in ((first_place, first_gate), (second_place, second_gate)):
            pick = jnp.where(place == col + c * 128, 1.0, 0.0)[toks].astype(BF16)
            added += gate[toks] * (
                jnp.dot(pick, coarse, preferred_element_type=F32)
                + jnp.dot(pick, fine, preferred_element_type=F32)
            )
        scored[toks] += added

    def step(n, _):
        @pl.when(n < STEPS)
        def _():
            c = n // TILES

            @pl.when(n % TILES == 0)
            def _():
                hidden_units(c)

            @pl.when(n == 0)
            def _():
                pass_late(1)
                pass_far(1)

            @pl.when(n == 2)
            def _():
                pass_first(2)

            @pl.when(n == 6)
            def _():
                pass_near(2)

            @pl.when(n == 11)
            def _():
                pass_late(2)
                pass_far(2)

            cols = pl.ds(pl.multiple_of(tile_of(n) * TILE, TILE), TILE)
            acc[n % 3] = jnp.dot(hid[...], down_w[:, cols], preferred_element_type=F32)

            @pl.when(n >= RING)
            def _():
                pair_copy(n - RING).wait_send()

            pair_out[n % RING] = acc[n % 3, rows_at((1 - core) * 128, 128), :].astype(BF16)
            pair_copy(n).start()

        m = n - LAG_PAIR

        @pl.when((m >= 0) & (m < STEPS))
        def _():
            slot = m % RING
            pair_copy(m).wait_recv()
            chip_sum[m % KEEP] = acc[m % 3, rows_at(core * 128, 128), :] + pair_in[m].astype(F32)

            @pl.when(row_first(m))
            def _():
                @pl.when(m >= RING)
                def _():
                    rows_copy(m - RING).wait_send()

                for i in range(4):
                    rows_out[(m % TILES) // 4, i] = chip_sum[m % KEEP, rows_at(i * 32 + (1 - yh) * 16, 16), :].astype(BF16)
                rows_copy(m).start()

            @pl.when(jnp.logical_not(row_first(m)))
            def _():
                @pl.when(m >= RING)
                def _():
                    far_copy(m - RING).wait_send()
                    edge_copy(m - RING).wait_send()

                first_out[slot, 0] = chip_sum[m % KEEP, quarter(2), :].astype(BF16)
                far_copy(m).start()
                first_out[slot, 1] = chip_sum[m % KEEP, quarter(-way(m)), :].astype(BF16)
                edge_copy(m).start()

        p = n - LAG_FAR

        @pl.when((p >= 0) & (p < STEPS))
        def _():
            slot = p % RING

            @pl.when(row_first(p))
            def _():
                @pl.when(p >= RING)
                def _():
                    far_block(p - RING).wait_send()
                    edge_block(p - RING).wait_send()

                rows_copy(p).wait_recv()
                for i in range(4):
                    chip_sum[p % KEEP, rows_at(i * 32 + yh * 16, 16), :] += rows_in[row_place(p), i].astype(F32)
                first_out[slot, 0, top] = chip_sum[p % KEEP, own_block(2), :].astype(BF16)
                far_block(p).start()
                first_out[slot, 1, top] = chip_sum[p % KEEP, own_block(-way(p)), :].astype(BF16)
                edge_block(p).start()

            @pl.when(jnp.logical_not(row_first(p)))
            def _():
                @pl.when(p >= RING)
                def _():
                    near_copy(p - RING).wait_send()

                far_copy(p).wait_recv()
                second_out[slot] = (
                    chip_sum[p % KEEP, quarter(way(p)), :] + far_in[p].astype(F32)
                ).astype(BF16)
                near_copy(p).start()

        q = n - LAG_NEAR

        @pl.when((q >= 0) & (q < STEPS))
        def _():
            slot = q % RING

            @pl.when(row_first(q))
            def _():
                @pl.when(q >= RING)
                def _():
                    near_block(q - RING).wait_send()

                far_block(q).wait_recv()
                second_out[slot, top] = (
                    chip_sum[q % KEEP, own_block(way(q)), :] + far_in[q, top].astype(F32)
                ).astype(BF16)
                near_block(q).start()
                row_sum[slot, top] = chip_sum[q % KEEP, own_block(0), :]

            @pl.when(jnp.logical_not(row_first(q)))
            def _():
                @pl.when(q >= RING)
                def _():
                    row_copy(q - RING).wait_send()

                edge_copy(q).wait_recv()
                near_copy(q).wait_recv()
                row_sum[slot] = (
                    chip_sum[q % KEEP, quarter(0), :]
                    + near_in[q, 0].astype(F32)
                    + near_in[q, 1].astype(F32)
                )
                row_out[slot] = row_sum[slot, rows_at((1 - yh) * 16, 16), :].astype(BF16)
                row_copy(q).start()

        r = n - LAG_ROW

        @pl.when(r >= 0)
        def _():
            slot = r % RING

            def hand_out(total):
                @pl.when(r >= RING)
                def _():
                    last_copy(r - RING, s, tile_of(r)).wait_send()

                last_out[slot] = total
                last_copy(r, s, tile_of(r)).start()

            @pl.when(row_first(r))
            def _():
                edge_block(r).wait_recv()
                near_block(r).wait_recv()
                hand_out(
                    row_sum[slot, top] + near_in[r, 0, top].astype(F32) + near_in[r, 1, top].astype(F32)
                )

            @pl.when(jnp.logical_not(row_first(r)))
            def _():
                row_copy(r).wait_recv()
                total = row_sum[slot, rows_at(yh * 16, 16), :] + row_in[r].astype(F32)

                @pl.when(r % TILES == TILES - 1)
                def _():
                    last_in[r // TILES, rows_at(s * 16, 16), :] = total

                @pl.when(r % TILES != TILES - 1)
                def _():
                    hand_out(total)

        for c in range(CHUNKS - 1):

            @pl.when(n == (c + 1) * TILES + LAG_ROW + 3)
            def _():
                combine(c)

        return 0

    lax.fori_loop(0, STEPS + LAG_ROW, step, 0)

    combine(CHUNKS - 1)
    out_ref[...] = scored[...].astype(BF16)

    for c in range(CHUNKS):
        for kind in range(16):
            gather(c, kind).wait_send()

    def drain(i, _):
        n = STEPS - RING + i
        pair_copy(n).wait_send()

        @pl.when(row_first(n))
        def _():
            rows_copy(n).wait_send()
            far_block(n).wait_send()
            edge_block(n).wait_send()
            near_block(n).wait_send()

        @pl.when(jnp.logical_not(row_first(n)))
        def _():
            far_copy(n).wait_send()
            edge_copy(n).wait_send()
            near_copy(n).wait_send()
            row_copy(n).wait_send()

        @pl.when(i < RING - 1)
        def _():
            last_copy(n, s, tile_of(n)).wait_send()

        return 0

    lax.fori_loop(0, RING, drain, 0)


def per_device(tokens, norm_gain, router_weight, expert_ids, w_gate, w_up, w_down):
    vmem = pl.BlockSpec(memory_space=pltpu.VMEM)
    anywhere = pl.BlockSpec(memory_space=pl.ANY)
    dma = pltpu.SemaphoreType.DMA
    out = pl.pallas_call(
        kernel,
        out_shape=jax.ShapeDtypeStruct((TOK, TILE), BF16),
        in_specs=[vmem] * 4 + [anywhere] * 3,
        out_specs=vmem,
        scratch_shapes=[
            pltpu.VMEM((D, UNITS), BF16),
            pltpu.VMEM((D, UNITS), BF16),
            pltpu.VMEM((UNITS, D), BF16),
            pltpu.VMEM((TOK, D), BF16),
            pltpu.VMEM((CHUNKS, ROWS, D), BF16),
            pltpu.VMEM((ROWS, UNITS), BF16),
            pltpu.VMEM((3, ROWS, TILE), F32),
            pltpu.VMEM((RING, 128, TILE), BF16),
            pltpu.VMEM((STEPS, 128, TILE), BF16),
            pltpu.VMEM((KEEP, 128, TILE), F32),
            pltpu.VMEM((RING, 2, 32, TILE), BF16),
            pltpu.VMEM((STEPS, 32, TILE), BF16),
            pltpu.VMEM((RING, 32, TILE), BF16),
            pltpu.VMEM((STEPS, 2, 32, TILE), BF16),
            pltpu.VMEM((RING, 32, TILE), F32),
            pltpu.VMEM((RING, 16, TILE), BF16),
            pltpu.VMEM((STEPS, 16, TILE), BF16),
            pltpu.VMEM((ROW_TILES, 4, 16, TILE), BF16),
            pltpu.VMEM((CHUNKS * ROW_TILES, 4, 16, TILE), BF16),
            pltpu.VMEM((RING, 16, TILE), F32),
            pltpu.VMEM((CHUNKS, 128, TILE), F32),
            pltpu.VMEM((TOK, TILE), F32),
            dma((3,)),
            dma((CHUNKS, 16)), dma((CHUNKS, 16)),
            dma((RING,)), dma((STEPS,)),
            dma((RING,)), dma((STEPS,)),
            dma((RING,)), dma((RING,)), dma((STEPS, 2)),
            dma((RING,)), dma((STEPS,)),
            dma((ROW_TILES,)), dma((CHUNKS * ROW_TILES,)),
            dma((RING,)), dma((CHUNKS, 8)),
        ],
        compiler_params=pltpu.CompilerParams(
            collective_id=0, has_side_effects=True, vmem_limit_bytes=61 * 2**20
        ),
        cost_estimate=pl.CostEstimate(flops=15 * 10**9, bytes_accessed=22 * 10**6, transcendentals=0),
    )(
        tokens.reshape(TOK, D), norm_gain, router_weight.T, expert_ids.transpose(0, 2, 1),
        w_gate[0], w_up[0], w_down[0],
    )
    return out.reshape(4, 32, TILE)


def solution(mesh):
    placed = (
        P(None, "dp", None),
        P(),
        P(),
        P(None, "dp", None),
        P("segment", None, "dp"),
        P("segment", None, "dp"),
        P("segment", "dp", None),
    )
    return jax.shard_map(
        per_device, mesh=mesh, in_specs=placed, out_specs=P(None, "dp", "segment"), check_vma=False
    )
```

```python
import functools

import jax
import jax.numpy as jnp
from jax import lax
from jax.experimental import pallas as pl
from jax.experimental.pallas import tpu as pltpu
from jax.sharding import PartitionSpec as P

MESH = pl.DeviceIdType.MESH
F32 = jnp.float32
BF16 = jnp.bfloat16
EPSILON = 1e-05

D = 6144
UNITS = 512
TOK = 128
CAP = 12
CHUNKS = 3
ROWS = 256
TILE = 768
TILES = D // TILE
STEPS = CHUNKS * TILES
RING = 8
KEEP = 12
LAG_PAIR, LAG_FAR, LAG_NEAR, LAG_ROW = 2, 6, 10, 14
HALF = D // 2
LATE = 2560
MIDDLE = (D + LATE) // 2
ROW_TILES = 2


def rows_at(ref_index, count):
    return pl.ds(pl.multiple_of(ref_index, 16), count)


def kernel(
    tok_ref, gain_ref, router_ref, ids_ref, gate_hbm, up_hbm, down_hbm, out_ref,
    gate_w, up_w, down_w, normed, x_buf, hid, acc, pair_out, pair_in, chip_sum,
    first_out, far_in, second_out, near_in, row_sum, row_out, row_in, rows_out, rows_in,
    last_out, last_in, scored,
    load_sem, ag_send, ag_recv, pair_s, pair_r, far_s, far_r, edge_s, near_s, near_r,
    row_s, row_r, rows_s, rows_r, last_s, last_r,
):
    s = lax.axis_index("segment")
    d = lax.axis_index("dp")
    core = d % 2
    x = (d // 2) % 4
    yh = d // 8

    def at_x(shift):
        return (s, yh * 8 + ((x + shift + 4) % 4) * 2 + core)

    across = (s, (d + 8) % 16)
    sibling = (s, yh * 8 + x * 2 + 1 - core)

    loads = [
        pltpu.make_async_copy(gate_hbm, gate_w, load_sem.at[0]),
        pltpu.make_async_copy(up_hbm, up_w, load_sem.at[1]),
        pltpu.make_async_copy(down_hbm, down_w, load_sem.at[2]),
    ]
    barrier = pltpu.get_barrier_semaphore()
    partners = [at_x(1), at_x(-1), across, sibling] + [((s + j) % 8, d) for j in range(1, 8)]
    for partner in partners:
        pl.semaphore_signal(barrier, inc=1, device_id=partner, device_id_type=MESH)
    for load in loads:
        load.start()

    def id_column(which):
        eye = lax.broadcasted_iota(jnp.int32, (32, 32), 0) == lax.broadcasted_iota(
            jnp.int32, (32, 32), 1
        )
        columns = [
            jnp.sum(
                jnp.where(eye, ids_ref[m, which : which + 1, :].astype(F32), 0.0),
                axis=-1,
                keepdims=True,
            )
            for m in range(4)
        ]
        return jnp.concatenate(columns, axis=0).astype(jnp.int32)

    first_id = id_column(0)
    second_id = id_column(1)
    expert = lax.broadcasted_iota(jnp.int32, (TOK, 8), 1)
    chosen = ((first_id == expert) | (second_id == expert)).astype(F32)
    row = lax.broadcasted_iota(jnp.int32, (TOK, TOK), 0)
    col = lax.broadcasted_iota(jnp.int32, (TOK, TOK), 1)
    earlier = ((col < row) & ((col >> 5) == (row >> 5))).astype(F32)
    position = jnp.dot(
        earlier.astype(BF16), chosen.astype(BF16), preferred_element_type=F32
    )
    micro_base = ((lax.broadcasted_iota(jnp.int32, (TOK, 1), 0) >> 5) * CAP).astype(F32)
    own_slot = micro_base + jnp.sum(
        jnp.where(expert == s, position, 0.0), axis=-1, keepdims=True
    )
    named_here = (first_id == s) | (second_id == s)
    slot_range = col.astype(F32)
    dispatch = jnp.where(named_here & (own_slot == slot_range), 1.0, 0.0).T

    def norm(first, count):
        gain = gain_ref[...].astype(F32).reshape(1, D)

        def norm_rows(i, _):
            at = rows_at(first + i * 16, 16)
            wide = tok_ref[at, :].astype(F32)
            inverse = lax.rsqrt(jnp.mean(wide * wide, axis=-1, keepdims=True) + EPSILON)
            normed[at, :] = (wide * inverse * gain).astype(BF16)
            return 0

        lax.fori_loop(0, count // 16, norm_rows, 0)

    own_row = core * 128 + x * 32 + yh * 16

    def route(c):
        pick = dispatch[c * 16 : (c + 1) * 16, c * 32 : c * 32 + 64].astype(BF16)

        def columns(j, _):
            cols = pl.ds(pl.multiple_of(j * TILE, TILE), TILE)
            x_buf[c, rows_at(own_row, 16), cols] = jnp.dot(
                pick, normed[c * 32 : c * 32 + 64, cols], preferred_element_type=F32
            ).astype(BF16)
            return 0

        lax.fori_loop(0, TILES, columns, 0)

    def pair_of(shift):
        return core * 128 + ((x + shift + 4) % 4) * 32

    def gather(c, kind):
        def block(shift, row):
            return x_buf.at[c, rows_at(pair_of(shift) + row * 16, 16)]

        def part(shift, row, start, stop):
            return x_buf.at[c, rows_at(pair_of(shift) + row * 16, 16), pl.ds(start, stop - start)]

        def pair(shift):
            return x_buf.at[c, rows_at(pair_of(shift), 32)]

        ref, to = {
            0: lambda: (block(0, yh), at_x(1)),
            1: lambda: (block(0, yh), at_x(-1)),
            2: lambda: (block(0, yh), across),
            3: lambda: (part(0, 1 - yh, LATE, D), at_x(1)),
            4: lambda: (part(0, 1 - yh, LATE, D), at_x(-1)),
            5: lambda: (part(-1, yh, 0, HALF), at_x(1)),
            6: lambda: (part(1, yh, HALF, D), at_x(-1)),
            7: lambda: (part(-1, 1 - yh, LATE, MIDDLE), at_x(1)),
            8: lambda: (part(1, 1 - yh, MIDDLE, D), at_x(-1)),
            9: lambda: (part(-1, yh, 0, LATE), across),
            10: lambda: (part(1, yh, 0, LATE), across),
            11: lambda: (part(2, yh, 0, LATE), across),
            12: lambda: (pair(0), sibling),
            13: lambda: (pair(-1), sibling),
            14: lambda: (pair(1), sibling),
            15: lambda: (pair(2), sibling),
        }[kind]()
        return pltpu.make_async_remote_copy(
            src_ref=ref, dst_ref=ref, send_sem=ag_send.at[c, kind], recv_sem=ag_recv.at[c, kind],
            device_id=to, device_id_type=MESH,
        )

    def go_on(c, waits, starts):
        for kind in waits:
            gather(c, kind).wait_recv()
        for kind in starts:
            gather(c, kind).start()

    def own_rows(c):
        go_on(c, (), (0, 1, 2))

    def pass_first(c):
        go_on(c, (0,), (5, 9))
        go_on(c, (1,), (6, 10))
        go_on(c, (2,), (3, 4, 12))

    def pass_near(c):
        go_on(c, (3,), (7,))
        go_on(c, (4,), (8,))
        go_on(c, (5, 6), (11,))

    def pass_late(c):
        go_on(c, (9,), (13,))
        go_on(c, (10,), (14,))

    def pass_far(c):
        go_on(c, (7, 8, 11), (15,))

    def gathered(c):
        go_on(c, (12, 13, 14, 15), ())

    norm(0, 64)
    route(0)
    pl.semaphore_wait(barrier, len(partners))
    own_rows(0)
    norm(64, 32)
    route(1)
    norm(96, 32)
    route(2)

    logits = lax.dot_general(
        normed[...], router_ref[...], (((1,), (1,)), ((), ())), preferred_element_type=F32
    )
    first_logit = jnp.sum(jnp.where(expert == first_id, logits, 0.0), axis=-1, keepdims=True)
    second_logit = jnp.sum(jnp.where(expert == second_id, logits, 0.0), axis=-1, keepdims=True)
    first_gate = jax.nn.sigmoid(first_logit - second_logit)
    second_gate = jax.nn.sigmoid(second_logit - first_logit)

    pass_first(0)
    own_rows(1)
    pass_near(0)
    pass_late(0)
    pass_far(0)
    pass_first(1)
    own_rows(2)

    for load in loads:
        load.wait()

    def remote(src, dst, send, recv, to):
        return pltpu.make_async_remote_copy(
            src_ref=src, dst_ref=dst, send_sem=send, recv_sem=recv, device_id=to, device_id_type=MESH
        )

    def way(n):
        return 1 - 2 * (n % 2)

    def pair_copy(n):
        return remote(pair_out.at[n % RING], pair_in.at[n], pair_s.at[n % RING], pair_r.at[n], sibling)

    def far_copy(n):
        return remote(first_out.at[n % RING, 0], far_in.at[n], far_s.at[n % RING], far_r.at[n], at_x(way(n)))

    def edge_copy(n):
        return remote(first_out.at[n % RING, 1], near_in.at[n, 1], edge_s.at[n % RING], near_r.at[n, 1], at_x(-way(n)))

    def near_copy(n):
        return remote(second_out.at[n % RING], near_in.at[n, 0], near_s.at[n % RING], near_r.at[n, 0], at_x(way(n)))

    def row_copy(n):
        return remote(row_out.at[n % RING], row_in.at[n], row_s.at[n % RING], row_r.at[n], across)

    def row_first(n):
        return (n % TILES == 2) | (n % TILES == 5)

    def row_place(n):
        return (n // TILES) * ROW_TILES + (n % TILES) // 4

    def rows_copy(n):
        return remote(rows_out.at[(n % TILES) // 4], rows_in.at[row_place(n)], rows_s.at[(n % TILES) // 4], rows_r.at[row_place(n)], across)

    top = pl.ds(0, 16)

    def far_block(n):
        return remote(first_out.at[n % RING, 0, top], far_in.at[n, top], far_s.at[n % RING], far_r.at[n], at_x(way(n)))

    def edge_block(n):
        return remote(first_out.at[n % RING, 1, top], near_in.at[n, 1, top], edge_s.at[n % RING], near_r.at[n, 1], at_x(-way(n)))

    def near_block(n):
        return remote(second_out.at[n % RING, top], near_in.at[n, 0, top], near_s.at[n % RING], near_r.at[n, 0], at_x(way(n)))

    def last_copy(n, source, to):
        c = n // TILES
        return remote(
            last_out.at[n % RING], last_in.at[c, rows_at(source * 16, 16)], last_s.at[n % RING],
            last_r.at[c, source], (to, d),
        )

    def tile_of(n):
        return (n % TILES + s + 1) % TILES

    def quarter(shift):
        return rows_at(((x + shift + 4) % 4) * 32, 32)

    def own_block(shift):
        return rows_at(((x + shift + 4) % 4) * 32 + yh * 16, 16)

    def hidden_units(c):
        gathered(c)

        def part(j, _):
            cols = pl.ds(pl.multiple_of(j * 256, 256), 256)
            rows = x_buf[c]
            g = jnp.dot(rows, gate_w[:, cols], preferred_element_type=F32)
            u = jnp.dot(rows, up_w[:, cols], preferred_element_type=F32)
            hid[:, cols] = (g * jax.nn.sigmoid(g) * u).astype(BF16)
            return 0

        lax.fori_loop(0, UNITS // 256, part, 0)

    def place_of(expert_id):
        where = jnp.sum(jnp.where(expert == expert_id, position, 0.0), axis=-1, keepdims=True)
        slot = (micro_base + where).astype(jnp.int32)
        return (slot >> 4) * 128 + expert_id * 16 + (slot & 15)

    first_place = place_of(first_id)
    second_place = place_of(second_id)
    own_cols = pl.ds(pl.multiple_of(s * TILE, TILE), TILE)
    scored[...] = tok_ref[:, own_cols].astype(F32)

    def combine(c):
        for j in range(1, 8):
            last_copy(c * TILES, (s + j) % 8, s).wait_recv()
        block = last_in[c]
        coarse = block.astype(BF16)
        fine = (block - coarse.astype(F32)).astype(BF16)
        toks = slice(c * 32, c * 32 + 64)
        added = 0.0
        for place, gate in ((first_place, first_gate), (second_place, second_gate)):
            pick = jnp.where(place == col + c * 128, 1.0, 0.0)[toks].astype(BF16)
            added += gate[toks] * (
                jnp.dot(pick, coarse, preferred_element_type=F32)
                + jnp.dot(pick, fine, preferred_element_type=F32)
            )
        scored[toks] += added

    def step(n, _):
        @pl.when(n < STEPS)
        def _():
            c = n // TILES

            @pl.when(n % TILES == 0)
            def _():
                hidden_units(c)

            @pl.when(n == 0)
            def _():
                pass_near(1)

            @pl.when(n == 3)
            def _():
                pass_late(1)
                pass_far(1)

            @pl.when(n == 5)
            def _():
                pass_first(2)

            @pl.when(n == 9)
            def _():
                pass_near(2)

            @pl.when(n == 13)
            def _():
                pass_late(2)
                pass_far(2)

            cols = pl.ds(pl.multiple_of(tile_of(n) * TILE, TILE), TILE)
            acc[n % 3] = jnp.dot(hid[...], down_w[:, cols], preferred_element_type=F32)

            @pl.when(n >= RING)
            def _():
                pair_copy(n - RING).wait_send()

            pair_out[n % RING] = acc[n % 3, rows_at((1 - core) * 128, 128), :].astype(BF16)
            pair_copy(n).start()

        m = n - LAG_PAIR

        @pl.when((m >= 0) & (m < STEPS))
        def _():
            slot = m % RING
            pair_copy(m).wait_recv()
            chip_sum[m % KEEP] = acc[m % 3, rows_at(core * 128, 128), :] + pair_in[m].astype(F32)

            @pl.when(row_first(m))
            def _():
                @pl.when(m >= RING)
                def _():
                    rows_copy(m - RING).wait_send()

                for i in range(4):
                    rows_out[(m % TILES) // 4, i] = chip_sum[m % KEEP, rows_at(i * 32 + (1 - yh) * 16, 16), :].astype(BF16)
                rows_copy(m).start()

            @pl.when(jnp.logical_not(row_first(m)))
            def _():
                @pl.when(m >= RING)
                def _():
                    far_copy(m - RING).wait_send()
                    edge_copy(m - RING).wait_send()

                first_out[slot, 0] = chip_sum[m % KEEP, quarter(2), :].astype(BF16)
                far_copy(m).start()
                first_out[slot, 1] = chip_sum[m % KEEP, quarter(-way(m)), :].astype(BF16)
                edge_copy(m).start()

        p = n - LAG_FAR

        @pl.when((p >= 0) & (p < STEPS))
        def _():
            slot = p % RING

            @pl.when(row_first(p))
            def _():
                @pl.when(p >= RING)
                def _():
                    far_block(p - RING).wait_send()
                    edge_block(p - RING).wait_send()

                rows_copy(p).wait_recv()
                for i in range(4):
                    chip_sum[p % KEEP, rows_at(i * 32 + yh * 16, 16), :] += rows_in[row_place(p), i].astype(F32)
                first_out[slot, 0, top] = chip_sum[p % KEEP, own_block(2), :].astype(BF16)
                far_block(p).start()
                first_out[slot, 1, top] = chip_sum[p % KEEP, own_block(-way(p)), :].astype(BF16)
                edge_block(p).start()

            @pl.when(jnp.logical_not(row_first(p)))
            def _():
                @pl.when(p >= RING)
                def _():
                    near_copy(p - RING).wait_send()

                far_copy(p).wait_recv()
                second_out[slot] = (
                    chip_sum[p % KEEP, quarter(way(p)), :] + far_in[p].astype(F32)
                ).astype(BF16)
                near_copy(p).start()

        q = n - LAG_NEAR

        @pl.when((q >= 0) & (q < STEPS))
        def _():
            slot = q % RING

            @pl.when(row_first(q))
            def _():
                @pl.when(q >= RING)
                def _():
                    near_block(q - RING).wait_send()

                far_block(q).wait_recv()
                second_out[slot, top] = (
                    chip_sum[q % KEEP, own_block(way(q)), :] + far_in[q, top].astype(F32)
                ).astype(BF16)
                near_block(q).start()
                row_sum[slot, top] = chip_sum[q % KEEP, own_block(0), :]

            @pl.when(jnp.logical_not(row_first(q)))
            def _():
                @pl.when(q >= RING)
                def _():
                    row_copy(q - RING).wait_send()

                edge_copy(q).wait_recv()
                near_copy(q).wait_recv()
                row_sum[slot] = (
                    chip_sum[q % KEEP, quarter(0), :]
                    + near_in[q, 0].astype(F32)
                    + near_in[q, 1].astype(F32)
                )
                row_out[slot] = row_sum[slot, rows_at((1 - yh) * 16, 16), :].astype(BF16)
                row_copy(q).start()

        r = n - LAG_ROW

        @pl.when(r >= 0)
        def _():
            slot = r % RING

            def hand_out(total):
                @pl.when(r >= RING)
                def _():
                    last_copy(r - RING, s, tile_of(r)).wait_send()

                last_out[slot] = total
                last_copy(r, s, tile_of(r)).start()

            @pl.when(row_first(r))
            def _():
                edge_block(r).wait_recv()
                near_block(r).wait_recv()
                hand_out(
                    row_sum[slot, top] + near_in[r, 0, top].astype(F32) + near_in[r, 1, top].astype(F32)
                )

            @pl.when(jnp.logical_not(row_first(r)))
            def _():
                row_copy(r).wait_recv()
                total = row_sum[slot, rows_at(yh * 16, 16), :] + row_in[r].astype(F32)

                @pl.when(r % TILES == TILES - 1)
                def _():
                    last_in[r // TILES, rows_at(s * 16, 16), :] = total

                @pl.when(r % TILES != TILES - 1)
                def _():
                    hand_out(total)

        for c in range(CHUNKS - 1):

            @pl.when(n == (c + 1) * TILES + LAG_ROW + 3)
            def _():
                combine(c)

        return 0

    lax.fori_loop(0, STEPS + LAG_ROW, step, 0)

    combine(CHUNKS - 1)
    out_ref[...] = scored[...].astype(BF16)

    for c in range(CHUNKS):
        for kind in range(16):
            gather(c, kind).wait_send()

    def drain(i, _):
        n = STEPS - RING + i
        pair_copy(n).wait_send()

        @pl.when(row_first(n))
        def _():
            rows_copy(n).wait_send()
            far_block(n).wait_send()
            edge_block(n).wait_send()
            near_block(n).wait_send()

        @pl.when(jnp.logical_not(row_first(n)))
        def _():
            far_copy(n).wait_send()
            edge_copy(n).wait_send()
            near_copy(n).wait_send()
            row_copy(n).wait_send()

        @pl.when(i < RING - 1)
        def _():
            last_copy(n, s, tile_of(n)).wait_send()

        return 0

    lax.fori_loop(0, RING, drain, 0)


def per_device(tokens, norm_gain, router_weight, expert_ids, w_gate, w_up, w_down):
    vmem = pl.BlockSpec(memory_space=pltpu.VMEM)
    anywhere = pl.BlockSpec(memory_space=pl.ANY)
    dma = pltpu.SemaphoreType.DMA
    out = pl.pallas_call(
        kernel,
        out_shape=jax.ShapeDtypeStruct((TOK, TILE), BF16),
        in_specs=[vmem] * 4 + [anywhere] * 3,
        out_specs=vmem,
        scratch_shapes=[
            pltpu.VMEM((D, UNITS), BF16),
            pltpu.VMEM((D, UNITS), BF16),
            pltpu.VMEM((UNITS, D), BF16),
            pltpu.VMEM((TOK, D), BF16),
            pltpu.VMEM((CHUNKS, ROWS, D), BF16),
            pltpu.VMEM((ROWS, UNITS), BF16),
            pltpu.VMEM((3, ROWS, TILE), F32),
            pltpu.VMEM((RING, 128, TILE), BF16),
            pltpu.VMEM((STEPS, 128, TILE), BF16),
            pltpu.VMEM((KEEP, 128, TILE), F32),
            pltpu.VMEM((RING, 2, 32, TILE), BF16),
            pltpu.VMEM((STEPS, 32, TILE), BF16),
            pltpu.VMEM((RING, 32, TILE), BF16),
            pltpu.VMEM((STEPS, 2, 32, TILE), BF16),
            pltpu.VMEM((RING, 32, TILE), F32),
            pltpu.VMEM((RING, 16, TILE), BF16),
            pltpu.VMEM((STEPS, 16, TILE), BF16),
            pltpu.VMEM((ROW_TILES, 4, 16, TILE), BF16),
            pltpu.VMEM((CHUNKS * ROW_TILES, 4, 16, TILE), BF16),
            pltpu.VMEM((RING, 16, TILE), F32),
            pltpu.VMEM((CHUNKS, 128, TILE), F32),
            pltpu.VMEM((TOK, TILE), F32),
            dma((3,)),
            dma((CHUNKS, 16)), dma((CHUNKS, 16)),
            dma((RING,)), dma((STEPS,)),
            dma((RING,)), dma((STEPS,)),
            dma((RING,)), dma((RING,)), dma((STEPS, 2)),
            dma((RING,)), dma((STEPS,)),
            dma((ROW_TILES,)), dma((CHUNKS * ROW_TILES,)),
            dma((RING,)), dma((CHUNKS, 8)),
        ],
        compiler_params=pltpu.CompilerParams(
            collective_id=0, has_side_effects=True, vmem_limit_bytes=61 * 2**20
        ),
        cost_estimate=pl.CostEstimate(flops=15 * 10**9, bytes_accessed=22 * 10**6, transcendentals=0),
    )(
        tokens.reshape(TOK, D), norm_gain, router_weight.T, expert_ids.transpose(0, 2, 1),
        w_gate[0], w_up[0], w_down[0],
    )
    return out.reshape(4, 32, TILE)


def solution(mesh):
    placed = (
        P(None, "dp", None),
        P(),
        P(),
        P(None, "dp", None),
        P("segment", None, "dp"),
        P("segment", None, "dp"),
        P("segment", "dp", None),
    )
    return jax.shard_map(
        per_device, mesh=mesh, in_specs=placed, out_specs=P(None, "dp", "segment"), check_vma=False
    )
```

```python
import functools

import jax
import jax.numpy as jnp
from jax import lax
from jax.experimental import pallas as pl
from jax.experimental.pallas import tpu as pltpu
from jax.sharding import PartitionSpec as P

MESH = pl.DeviceIdType.MESH
F32 = jnp.float32
BF16 = jnp.bfloat16
EPSILON = 1e-05

D = 6144
UNITS = 512
TOK = 128
CAP = 12
CHUNKS = 3
ROWS = 256
TILE = 768
TILES = D // TILE
STEPS = CHUNKS * TILES
RING = 8
KEEP = 12
LAG_PAIR, LAG_FAR, LAG_NEAR, LAG_ROW = 2, 6, 10, 14
HALF = D // 2
LATE = 2560
MIDDLE = (D + LATE) // 2
ROW_TILES = 2


def rows_at(ref_index, count):
    return pl.ds(pl.multiple_of(ref_index, 16), count)


def kernel(
    tok_ref, gain_ref, router_ref, ids_ref, gate_hbm, up_hbm, down_hbm, out_ref,
    gate_w, up_w, down_w, normed, x_buf, hid, acc, pair_out, pair_in, chip_sum,
    first_out, far_in, second_out, near_in, row_sum, row_out, row_in, rows_out, rows_in,
    last_out, last_in, scored,
    load_sem, ag_send, ag_recv, pair_s, pair_r, far_s, far_r, edge_s, near_s, near_r,
    row_s, row_r, rows_s, rows_r, last_s, last_r,
):
    s = lax.axis_index("segment")
    d = lax.axis_index("dp")
    core = d % 2
    x = (d // 2) % 4
    yh = d // 8

    def at_x(shift):
        return (s, yh * 8 + ((x + shift + 4) % 4) * 2 + core)

    across = (s, (d + 8) % 16)
    sibling = (s, yh * 8 + x * 2 + 1 - core)

    loads = [
        pltpu.make_async_copy(gate_hbm, gate_w, load_sem.at[0]),
        pltpu.make_async_copy(up_hbm, up_w, load_sem.at[1]),
        pltpu.make_async_copy(down_hbm, down_w, load_sem.at[2]),
    ]
    barrier = pltpu.get_barrier_semaphore()
    partners = [at_x(1), at_x(-1), across, sibling] + [((s + j) % 8, d) for j in range(1, 8)]
    for partner in partners:
        pl.semaphore_signal(barrier, inc=1, device_id=partner, device_id_type=MESH)
    for load in loads:
        load.start()

    def id_column(which):
        eye = lax.broadcasted_iota(jnp.int32, (32, 32), 0) == lax.broadcasted_iota(
            jnp.int32, (32, 32), 1
        )
        columns = [
            jnp.sum(
                jnp.where(eye, ids_ref[m, which : which + 1, :].astype(F32), 0.0),
                axis=-1,
                keepdims=True,
            )
            for m in range(4)
        ]
        return jnp.concatenate(columns, axis=0).astype(jnp.int32)

    first_id = id_column(0)
    second_id = id_column(1)
    expert = lax.broadcasted_iota(jnp.int32, (TOK, 8), 1)
    chosen = ((first_id == expert) | (second_id == expert)).astype(F32)
    row = lax.broadcasted_iota(jnp.int32, (TOK, TOK), 0)
    col = lax.broadcasted_iota(jnp.int32, (TOK, TOK), 1)
    earlier = ((col < row) & ((col >> 5) == (row >> 5))).astype(F32)
    position = jnp.dot(
        earlier.astype(BF16), chosen.astype(BF16), preferred_element_type=F32
    )
    micro_base = ((lax.broadcasted_iota(jnp.int32, (TOK, 1), 0) >> 5) * CAP).astype(F32)
    own_slot = micro_base + jnp.sum(
        jnp.where(expert == s, position, 0.0), axis=-1, keepdims=True
    )
    named_here = (first_id == s) | (second_id == s)
    slot_range = col.astype(F32)
    dispatch = jnp.where(named_here & (own_slot == slot_range), 1.0, 0.0).T

    def norm(first, count):
        gain = gain_ref[...].astype(F32).reshape(1, D)

        def norm_rows(i, _):
            at = rows_at(first + i * 16, 16)
            wide = tok_ref[at, :].astype(F32)
            inverse = lax.rsqrt(jnp.mean(wide * wide, axis=-1, keepdims=True) + EPSILON)
            normed[at, :] = (wide * inverse * gain).astype(BF16)
            return 0

        lax.fori_loop(0, count // 16, norm_rows, 0)

    own_row = core * 128 + x * 32 + yh * 16

    def route(c):
        pick = dispatch[c * 16 : (c + 1) * 16, c * 32 : c * 32 + 64].astype(BF16)

        def columns(j, _):
            cols = pl.ds(pl.multiple_of(j * TILE, TILE), TILE)
            x_buf[c, rows_at(own_row, 16), cols] = jnp.dot(
                pick, normed[c * 32 : c * 32 + 64, cols], preferred_element_type=F32
            ).astype(BF16)
            return 0

        lax.fori_loop(0, TILES, columns, 0)

    def pair_of(shift):
        return core * 128 + ((x + shift + 4) % 4) * 32

    def gather(c, kind):
        def block(shift, row):
            return x_buf.at[c, rows_at(pair_of(shift) + row * 16, 16)]

        def part(shift, row, start, stop):
            return x_buf.at[c, rows_at(pair_of(shift) + row * 16, 16), pl.ds(start, stop - start)]

        def pair(shift):
            return x_buf.at[c, rows_at(pair_of(shift), 32)]

        ref, to = {
            0: lambda: (block(0, yh), at_x(1)),
            1: lambda: (block(0, yh), at_x(-1)),
            2: lambda: (block(0, yh), across),
            3: lambda: (part(0, 1 - yh, LATE, D), at_x(1)),
            4: lambda: (part(0, 1 - yh, LATE, D), at_x(-1)),
            5: lambda: (part(-1, yh, 0, HALF), at_x(1)),
            6: lambda: (part(1, yh, HALF, D), at_x(-1)),
            7: lambda: (part(-1, 1 - yh, LATE, MIDDLE), at_x(1)),
            8: lambda: (part(1, 1 - yh, MIDDLE, D), at_x(-1)),
            9: lambda: (part(-1, yh, 0, LATE), across),
            10: lambda: (part(1, yh, 0, LATE), across),
            11: lambda: (part(2, yh, 0, LATE), across),
            12: lambda: (pair(0), sibling),
            13: lambda: (pair(-1), sibling),
            14: lambda: (pair(1), sibling),
            15: lambda: (pair(2), sibling),
        }[kind]()
        return pltpu.make_async_remote_copy(
            src_ref=ref, dst_ref=ref, send_sem=ag_send.at[c, kind], recv_sem=ag_recv.at[c, kind],
            device_id=to, device_id_type=MESH,
        )

    def go_on(c, waits, starts):
        for kind in waits:
            gather(c, kind).wait_recv()
        for kind in starts:
            gather(c, kind).start()

    def own_rows(c):
        go_on(c, (), (0, 1, 2))

    def pass_first(c):
        go_on(c, (2,), (3, 4, 12))
        go_on(c, (0,), (5, 9))
        go_on(c, (1,), (6, 10))

    def pass_near(c):
        go_on(c, (3,), (7,))
        go_on(c, (4,), (8,))
        go_on(c, (5, 6), (11,))

    def pass_late(c):
        go_on(c, (9,), (13,))
        go_on(c, (10,), (14,))

    def pass_far(c):
        go_on(c, (7, 8, 11), (15,))

    def gathered(c):
        go_on(c, (12, 13, 14, 15), ())

    norm(0, 64)
    route(0)
    pl.semaphore_wait(barrier, len(partners))
    own_rows(0)
    norm(64, 32)
    route(1)
    norm(96, 32)
    route(2)

    logits = lax.dot_general(
        normed[...], router_ref[...], (((1,), (1,)), ((), ())), preferred_element_type=F32
    )
    first_logit = jnp.sum(jnp.where(expert == first_id, logits, 0.0), axis=-1, keepdims=True)
    second_logit = jnp.sum(jnp.where(expert == second_id, logits, 0.0), axis=-1, keepdims=True)
    first_gate = jax.nn.sigmoid(first_logit - second_logit)
    second_gate = jax.nn.sigmoid(second_logit - first_logit)

    pass_first(0)
    own_rows(1)
    pass_near(0)
    pass_late(0)
    pass_far(0)
    pass_first(1)
    own_rows(2)

    for load in loads:
        load.wait()

    def remote(src, dst, send, recv, to):
        return pltpu.make_async_remote_copy(
            src_ref=src, dst_ref=dst, send_sem=send, recv_sem=recv, device_id=to, device_id_type=MESH
        )

    def way(n):
        return 1 - 2 * (n % 2)

    def pair_copy(n):
        return remote(pair_out.at[n % RING], pair_in.at[n], pair_s.at[n % RING], pair_r.at[n], sibling)

    def far_copy(n):
        return remote(first_out.at[n % RING, 0], far_in.at[n], far_s.at[n % RING], far_r.at[n], at_x(way(n)))

    def edge_copy(n):
        return remote(first_out.at[n % RING, 1], near_in.at[n, 1], edge_s.at[n % RING], near_r.at[n, 1], at_x(-way(n)))

    def near_copy(n):
        return remote(second_out.at[n % RING], near_in.at[n, 0], near_s.at[n % RING], near_r.at[n, 0], at_x(way(n)))

    def row_copy(n):
        return remote(row_out.at[n % RING], row_in.at[n], row_s.at[n % RING], row_r.at[n], across)

    def row_first(n):
        return (n % TILES == 2) | (n % TILES == 5)

    def row_place(n):
        return (n // TILES) * ROW_TILES + (n % TILES) // 4

    def rows_copy(n):
        return remote(rows_out.at[(n % TILES) // 4], rows_in.at[row_place(n)], rows_s.at[(n % TILES) // 4], rows_r.at[row_place(n)], across)

    top = pl.ds(0, 16)

    def far_block(n):
        return remote(first_out.at[n % RING, 0, top], far_in.at[n, top], far_s.at[n % RING], far_r.at[n], at_x(way(n)))

    def edge_block(n):
        return remote(first_out.at[n % RING, 1, top], near_in.at[n, 1, top], edge_s.at[n % RING], near_r.at[n, 1], at_x(-way(n)))

    def near_block(n):
        return remote(second_out.at[n % RING, top], near_in.at[n, 0, top], near_s.at[n % RING], near_r.at[n, 0], at_x(way(n)))

    def last_copy(n, source, to):
        c = n // TILES
        return remote(
            last_out.at[n % RING], last_in.at[c, rows_at(source * 16, 16)], last_s.at[n % RING],
            last_r.at[c, source], (to, d),
        )

    def tile_of(n):
        return (n % TILES + s + 1) % TILES

    def quarter(shift):
        return rows_at(((x + shift + 4) % 4) * 32, 32)

    def own_block(shift):
        return rows_at(((x + shift + 4) % 4) * 32 + yh * 16, 16)

    def hidden_units(c):
        gathered(c)

        def part(j, _):
            cols = pl.ds(pl.multiple_of(j * 256, 256), 256)
            rows = x_buf[c]
            g = jnp.dot(rows, gate_w[:, cols], preferred_element_type=F32)
            u = jnp.dot(rows, up_w[:, cols], preferred_element_type=F32)
            hid[:, cols] = (g * jax.nn.sigmoid(g) * u).astype(BF16)
            return 0

        lax.fori_loop(0, UNITS // 256, part, 0)

    def place_of(expert_id):
        where = jnp.sum(jnp.where(expert == expert_id, position, 0.0), axis=-1, keepdims=True)
        slot = (micro_base + where).astype(jnp.int32)
        return (slot >> 4) * 128 + expert_id * 16 + (slot & 15)

    first_place = place_of(first_id)
    second_place = place_of(second_id)
    own_cols = pl.ds(pl.multiple_of(s * TILE, TILE), TILE)
    scored[...] = tok_ref[:, own_cols].astype(F32)

    def combine(c):
        for j in range(1, 8):
            last_copy(c * TILES, (s + j) % 8, s).wait_recv()
        block = last_in[c]
        coarse = block.astype(BF16)
        fine = (block - coarse.astype(F32)).astype(BF16)
        toks = slice(c * 32, c * 32 + 64)
        added = 0.0
        for place, gate in ((first_place, first_gate), (second_place, second_gate)):
            pick = jnp.where(place == col + c * 128, 1.0, 0.0)[toks].astype(BF16)
            added += gate[toks] * (
                jnp.dot(pick, coarse, preferred_element_type=F32)
                + jnp.dot(pick, fine, preferred_element_type=F32)
            )
        scored[toks] += added

    def step(n, _):
        @pl.when(n < STEPS)
        def _():
            c = n // TILES

            @pl.when(n % TILES == 0)
            def _():
                hidden_units(c)

            @pl.when(n == 0)
            def _():
                pass_near(1)

            @pl.when(n == 3)
            def _():
                pass_late(1)
                pass_far(1)

            @pl.when(n == 5)
            def _():
                pass_first(2)

            @pl.when(n == 9)
            def _():
                pass_near(2)

            @pl.when(n == 13)
            def _():
                pass_late(2)
                pass_far(2)

            cols = pl.ds(pl.multiple_of(tile_of(n) * TILE, TILE), TILE)
            acc[n % 3] = jnp.dot(hid[...], down_w[:, cols], preferred_element_type=F32)

            @pl.when(n >= RING)
            def _():
                pair_copy(n - RING).wait_send()

            pair_out[n % RING] = acc[n % 3, rows_at((1 - core) * 128, 128), :].astype(BF16)
            pair_copy(n).start()

        m = n - LAG_PAIR

        @pl.when((m >= 0) & (m < STEPS))
        def _():
            slot = m % RING
            pair_copy(m).wait_recv()
            chip_sum[m % KEEP] = acc[m % 3, rows_at(core * 128, 128), :] + pair_in[m].astype(F32)

            @pl.when(row_first(m))
            def _():
                @pl.when(m >= RING)
                def _():
                    rows_copy(m - RING).wait_send()

                for i in range(4):
                    rows_out[(m % TILES) // 4, i] = chip_sum[m % KEEP, rows_at(i * 32 + (1 - yh) * 16, 16), :].astype(BF16)
                rows_copy(m).start()

            @pl.when(jnp.logical_not(row_first(m)))
            def _():
                @pl.when(m >= RING)
                def _():
                    far_copy(m - RING).wait_send()
                    edge_copy(m - RING).wait_send()

                first_out[slot, 0] = chip_sum[m % KEEP, quarter(2), :].astype(BF16)
                far_copy(m).start()
                first_out[slot, 1] = chip_sum[m % KEEP, quarter(-way(m)), :].astype(BF16)
                edge_copy(m).start()

        p = n - LAG_FAR

        @pl.when((p >= 0) & (p < STEPS))
        def _():
            slot = p % RING

            @pl.when(row_first(p))
            def _():
                @pl.when(p >= RING)
                def _():
                    far_block(p - RING).wait_send()
                    edge_block(p - RING).wait_send()

                rows_copy(p).wait_recv()
                for i in range(4):
                    chip_sum[p % KEEP, rows_at(i * 32 + yh * 16, 16), :] += rows_in[row_place(p), i].astype(F32)
                first_out[slot, 0, top] = chip_sum[p % KEEP, own_block(2), :].astype(BF16)
                far_block(p).start()
                first_out[slot, 1, top] = chip_sum[p % KEEP, own_block(-way(p)), :].astype(BF16)
                edge_block(p).start()

            @pl.when(jnp.logical_not(row_first(p)))
            def _():
                @pl.when(p >= RING)
                def _():
                    near_copy(p - RING).wait_send()

                far_copy(p).wait_recv()
                second_out[slot] = (
                    chip_sum[p % KEEP, quarter(way(p)), :] + far_in[p].astype(F32)
                ).astype(BF16)
                near_copy(p).start()

        q = n - LAG_NEAR

        @pl.when((q >= 0) & (q < STEPS))
        def _():
            slot = q % RING

            @pl.when(row_first(q))
            def _():
                @pl.when(q >= RING)
                def _():
                    near_block(q - RING).wait_send()

                far_block(q).wait_recv()
                second_out[slot, top] = (
                    chip_sum[q % KEEP, own_block(way(q)), :] + far_in[q, top].astype(F32)
                ).astype(BF16)
                near_block(q).start()
                row_sum[slot, top] = chip_sum[q % KEEP, own_block(0), :]

            @pl.when(jnp.logical_not(row_first(q)))
            def _():
                @pl.when(q >= RING)
                def _():
                    row_copy(q - RING).wait_send()

                edge_copy(q).wait_recv()
                near_copy(q).wait_recv()
                row_sum[slot] = (
                    chip_sum[q % KEEP, quarter(0), :]
                    + near_in[q, 0].astype(F32)
                    + near_in[q, 1].astype(F32)
                )
                row_out[slot] = row_sum[slot, rows_at((1 - yh) * 16, 16), :].astype(BF16)
                row_copy(q).start()

        r = n - LAG_ROW

        @pl.when(r >= 0)
        def _():
            slot = r % RING

            def hand_out(total):
                @pl.when(r >= RING)
                def _():
                    last_copy(r - RING, s, tile_of(r)).wait_send()

                last_out[slot] = total
                last_copy(r, s, tile_of(r)).start()

            @pl.when(row_first(r))
            def _():
                edge_block(r).wait_recv()
                near_block(r).wait_recv()
                hand_out(
                    row_sum[slot, top] + near_in[r, 0, top].astype(F32) + near_in[r, 1, top].astype(F32)
                )

            @pl.when(jnp.logical_not(row_first(r)))
            def _():
                row_copy(r).wait_recv()
                total = row_sum[slot, rows_at(yh * 16, 16), :] + row_in[r].astype(F32)

                @pl.when(r % TILES == TILES - 1)
                def _():
                    last_in[r // TILES, rows_at(s * 16, 16), :] = total

                @pl.when(r % TILES != TILES - 1)
                def _():
                    hand_out(total)

        for c in range(CHUNKS - 1):

            @pl.when(n == (c + 1) * TILES + LAG_ROW + 3)
            def _():
                combine(c)

        return 0

    lax.fori_loop(0, STEPS + LAG_ROW, step, 0)

    combine(CHUNKS - 1)
    out_ref[...] = scored[...].astype(BF16)

    for c in range(CHUNKS):
        for kind in range(16):
            gather(c, kind).wait_send()

    def drain(i, _):
        n = STEPS - RING + i
        pair_copy(n).wait_send()

        @pl.when(row_first(n))
        def _():
            rows_copy(n).wait_send()
            far_block(n).wait_send()
            edge_block(n).wait_send()
            near_block(n).wait_send()

        @pl.when(jnp.logical_not(row_first(n)))
        def _():
            far_copy(n).wait_send()
            edge_copy(n).wait_send()
            near_copy(n).wait_send()
            row_copy(n).wait_send()

        @pl.when(i < RING - 1)
        def _():
            last_copy(n, s, tile_of(n)).wait_send()

        return 0

    lax.fori_loop(0, RING, drain, 0)


def per_device(tokens, norm_gain, router_weight, expert_ids, w_gate, w_up, w_down):
    vmem = pl.BlockSpec(memory_space=pltpu.VMEM)
    anywhere = pl.BlockSpec(memory_space=pl.ANY)
    dma = pltpu.SemaphoreType.DMA
    out = pl.pallas_call(
        kernel,
        out_shape=jax.ShapeDtypeStruct((TOK, TILE), BF16),
        in_specs=[vmem] * 4 + [anywhere] * 3,
        out_specs=vmem,
        scratch_shapes=[
            pltpu.VMEM((D, UNITS), BF16),
            pltpu.VMEM((D, UNITS), BF16),
            pltpu.VMEM((UNITS, D), BF16),
            pltpu.VMEM((TOK, D), BF16),
            pltpu.VMEM((CHUNKS, ROWS, D), BF16),
            pltpu.VMEM((ROWS, UNITS), BF16),
            pltpu.VMEM((3, ROWS, TILE), F32),
            pltpu.VMEM((RING, 128, TILE), BF16),
            pltpu.VMEM((STEPS, 128, TILE), BF16),
            pltpu.VMEM((KEEP, 128, TILE), F32),
            pltpu.VMEM((RING, 2, 32, TILE), BF16),
            pltpu.VMEM((STEPS, 32, TILE), BF16),
            pltpu.VMEM((RING, 32, TILE), BF16),
            pltpu.VMEM((STEPS, 2, 32, TILE), BF16),
            pltpu.VMEM((RING, 32, TILE), F32),
            pltpu.VMEM((RING, 16, TILE), BF16),
            pltpu.VMEM((STEPS, 16, TILE), BF16),
            pltpu.VMEM((ROW_TILES, 4, 16, TILE), BF16),
            pltpu.VMEM((CHUNKS * ROW_TILES, 4, 16, TILE), BF16),
            pltpu.VMEM((RING, 16, TILE), F32),
            pltpu.VMEM((CHUNKS, 128, TILE), F32),
            pltpu.VMEM((TOK, TILE), F32),
            dma((3,)),
            dma((CHUNKS, 16)), dma((CHUNKS, 16)),
            dma((RING,)), dma((STEPS,)),
            dma((RING,)), dma((STEPS,)),
            dma((RING,)), dma((RING,)), dma((STEPS, 2)),
            dma((RING,)), dma((STEPS,)),
            dma((ROW_TILES,)), dma((CHUNKS * ROW_TILES,)),
            dma((RING,)), dma((CHUNKS, 8)),
        ],
        compiler_params=pltpu.CompilerParams(
            collective_id=0, has_side_effects=True, vmem_limit_bytes=61 * 2**20
        ),
        cost_estimate=pl.CostEstimate(flops=15 * 10**9, bytes_accessed=22 * 10**6, transcendentals=0),
    )(
        tokens.reshape(TOK, D), norm_gain, router_weight.T, expert_ids.transpose(0, 2, 1),
        w_gate[0], w_up[0], w_down[0],
    )
    return out.reshape(4, 32, TILE)


def solution(mesh):
    placed = (
        P(None, "dp", None),
        P(),
        P(),
        P(None, "dp", None),
        P("segment", None, "dp"),
        P("segment", None, "dp"),
        P("segment", "dp", None),
    )
    return jax.shard_map(
        per_device, mesh=mesh, in_specs=placed, out_specs=P(None, "dp", "segment"), check_vma=False
    )
```
